32 devices in a mesh: parts: 2 (over y), latent: 16 (over z, x, core).
Axes of the slice: x: 2, y: 2, z: 4, core: 2. Of those that a mesh axis runs over, the one named last changes fastest.
Arguments:
- residual: bfloat16 [512, 4608], P(('parts', 'latent')), parts along dimension 0, may hold values from -6 to 6
- enc_weight: bfloat16 [4608, 8192], P(None, 'latent'), may hold values from -0.09375 to 0.09375
- enc_bias: float32 [8192], P('latent'), may hold values from -3 to 3
- threshold: float32 [8192], P('latent'), may hold values from 0.3 to 2
- dec_weight: bfloat16 [8192, 4608], P('latent'), may hold values from -0.1875 to 0.1875
- dec_bias: float32 [4608], replicated, may hold values from -3 to 3
- pre_gain: float32 [4608], replicated, may hold values from 0.1 to 1.9
- gate_weight: bfloat16 [4608, 2304], P(None, 'latent'), may hold values from -0.09375 to 0.09375
- up_weight: bfloat16 [4608, 2304], P(None, 'latent'), may hold values from -0.09375 to 0.09375
- down_weight: bfloat16 [2304, 4608], P('latent'), may hold values from -0.125 to 0.125
- post_gain: float32 [4608], replicated, may hold values from 0.1 to 1.9
Outputs:
- spliced_out: bfloat16 [512, 4608], P(('parts', 'latent')), parts along dimension 0
The draws below stay inside these ranges and needn't reach their ends.
There are 2 independent parts, one for each index of `parts`. The reference program is written for one: setup_inputs(seed, part) draws one part's arguments, and reference() takes and returns one part's arrays. A program takes and returns all parts, laid end to end along the dimension named above; an argument that names none is the same for every part. Nothing has to cross between parts.
All inputs are finite; a program needn't handle non-finite values.
Results may differ from the reference program's by a relative error of at most 0.0057.
Values may be sent and summed in bfloat16 or wider, within the bound.
A program may use at most 128 MiB of HBM per device.

```python
import math
import jax
import jax.numpy as jnp
from jax import lax

D = 4608
TOK = 256
LATENTS = 8192
FF = 2304


def with_spikes(array, stream_key, source, target, blocks, factor):
    owner, partner = [(jnp.arange(array.shape[position]) // (array.shape[position] // blocks)).reshape([-1 if axis == position else 1 for axis in range(array.ndim)]) for position in (source, target)]
    chosen = jax.random.permutation(stream_key, blocks)[partner]
    strong = (owner == chosen) | (owner == (partner + blocks // 2) % blocks)
    return jnp.where(strong, factor * array, array)


def level_of(stream_key, extent, cuts, smallest, top_value):
    level, own = 1.0, jax.random.fold_in(stream_key, 6)
    for dim, blocks in cuts:
        draws = jnp.exp(jax.random.uniform(jax.random.fold_in(own, dim), (blocks,), jnp.float32, smallest / len(cuts), top_value / len(cuts)))
        level = level * jnp.repeat(draws, extent[dim] // blocks).reshape([-1 if axis == dim else 1 for axis in range(len(extent))])
    return level


def bell_draw(rng, shape, spread, most, cuts=(), held_as=jnp.bfloat16):
    level = level_of(rng, shape, cuts, -0.22, 0.18) if cuts else 1.0
    entries = jax.random.normal(rng, shape, jnp.float32) * spread * level
    return jnp.minimum(jnp.maximum(entries, -most), most).astype(held_as)


def noise_with(stream_key, shape, scale, bound, pieces, heavy, dtype=jnp.bfloat16):
    array = scale * jax.random.normal(stream_key, shape, jnp.float32)
    if pieces:
        array = array * level_of(stream_key, shape, pieces, -0.22, 0.18)
    return jnp.clip(with_spikes(array, jax.random.fold_in(stream_key, 3), *heavy), -bound, bound).astype(dtype)


def setup_inputs(seed: int = 0, part: int = 0) -> dict:
    key_list = jax.random.split(jax.random.key(seed), 12)
    own_keys = jax.random.split(jax.random.fold_in(key_list[11], part), 12)
    return {
        "residual": bell_draw(own_keys[0], (TOK, D), 1.0, 6.0, ((0, 16),)),
        "enc_weight": bell_draw(key_list[1], (D, LATENTS), D ** -0.5, 0.09375, ((1, 16),)),
        "enc_bias": bell_draw(key_list[2], (LATENTS,), 0.5, 3.0, ((0, 16),), jnp.float32),
        "threshold": jnp.clip(jnp.exp(math.log(2.0) - 1.89712 * jax.random.uniform(key_list[3], (LATENTS,), jnp.float32) ** level_of(key_list[3], (LATENTS,), ((0, 16),), -0.2, 0.2)), 0.3, 2.0),
        "dec_weight": noise_with(key_list[4], (LATENTS, D), (LATENTS // 4) ** -0.5, 0.1875, ((0, 16),), (0, 1, 16, 2.0)),
        "dec_bias": bell_draw(key_list[5], (D,), 0.5, 3.0, (), jnp.float32),
        "pre_gain": jnp.clip(1.0 + 0.18 * jax.random.normal(key_list[6], (D,), jnp.float32), 0.1, 1.9),
        "gate_weight": bell_draw(key_list[7], (D, FF), D ** -0.5, 0.09375, ((1, 16),)),
        "up_weight": bell_draw(key_list[8], (D, FF), D ** -0.5, 0.09375, ((1, 16),)),
        "down_weight": bell_draw(key_list[9], (FF, D), FF ** -0.5, 0.125, ((0, 16),)),
        "post_gain": jnp.clip(1.0 + 0.18 * jax.random.normal(key_list[10], (D,), jnp.float32), 0.1, 1.9),
    }


sharpness = 10.0
epsilon = 1e-06

def rms_scale(values, gain):
    return values * jax.lax.rsqrt(lax.optimization_barrier(jnp.mean(values * values, axis=-1, keepdims=True)) + epsilon) * gain

def reference(residual, enc_weight, enc_bias, threshold, dec_weight, dec_bias, pre_gain, gate_weight, up_weight, down_weight, post_gain):
    preact = jnp.dot(residual, enc_weight, preferred_element_type=jnp.float32) + enc_bias
    latent_acts = (preact * jax.nn.sigmoid(sharpness * (preact - threshold))).astype(jnp.bfloat16)
    rebuilt = jnp.dot(latent_acts, dec_weight, preferred_element_type=jnp.float32) + dec_bias
    normed = rms_scale(rebuilt, pre_gain).astype(jnp.bfloat16)
    gate_proj = jnp.dot(normed, gate_weight, preferred_element_type=jnp.float32)
    up_proj = jnp.dot(normed, up_weight, preferred_element_type=jnp.float32)
    hidden = (jax.nn.gelu(gate_proj, approximate=True) * up_proj).astype(jnp.bfloat16)
    ffn_sum = jnp.dot(hidden, down_weight, preferred_element_type=jnp.float32)
    return (rebuilt + rms_scale(ffn_sum, post_gain)).astype(jnp.bfloat16)
```

```python
import functools

import jax
import jax.numpy as jnp
from jax import lax
from jax.experimental import pallas as pl
from jax.experimental.pallas import tpu as pltpu
from jax.sharding import PartitionSpec as P

sharpness = 10.0
epsilon = 1e-06
MESH = pl.DeviceIdType.MESH
f32 = jnp.float32
bf16 = jnp.bfloat16


def rms_scale(values, gain):
    return values * lax.rsqrt(jnp.mean(values * values, axis=-1, keepdims=True) + epsilon) * gain


def plain_device(
    residual,
    enc_weight,
    enc_bias,
    threshold,
    dec_weight,
    dec_bias,
    pre_gain,
    gate_weight,
    up_weight,
    down_weight,
    post_gain,
):
    def encode(block_rows):
        preact = jnp.dot(block_rows, enc_weight, preferred_element_type=f32) + enc_bias
        return (preact * jax.nn.sigmoid(sharpness * (preact - threshold))).astype(bf16)

    def feed_hidden(block_rows):
        gate_proj = jnp.dot(block_rows, gate_weight, preferred_element_type=f32)
        up_proj = jnp.dot(block_rows, up_weight, preferred_element_type=f32)
        return (jax.nn.gelu(gate_proj, approximate=True) * up_proj).astype(bf16)

    def scatter_sum(lhs, rhs):
        return lax.psum_scatter(
            jnp.dot(lhs, rhs, preferred_element_type=f32), "latent", scatter_dimension=0, tiled=True
        )

    latent_acts = encode(lax.all_gather(residual, "latent", axis=0, tiled=True))
    rebuilt = scatter_sum(latent_acts, dec_weight) + dec_bias
    normed = rms_scale(rebuilt, pre_gain).astype(bf16)
    hidden = feed_hidden(lax.all_gather(normed, "latent", axis=0, tiled=True))
    ffn_sum = scatter_sum(hidden, down_weight)
    return (rebuilt + rms_scale(ffn_sum, post_gain)).astype(bf16)


def chunk_of(extent):
    for pieces in (6, 4, 8, 2):
        if extent % (128 * pieces) == 0:
            return extent // pieces
    return extent


def kernel(
    Z,
    rows,
    res_ref,
    enc_hbm,
    bias_ref,
    thr_ref,
    dec_hbm,
    dec_bias_ref,
    pre_gain_ref,
    gate_hbm,
    up_hbm,
    down_hbm,
    post_gain_ref,
    out_ref,
    enc_w,
    dec_w,
    gate_w,
    up_w,
    down_w,
    gath1,
    gath2,
    own_part,
    sib_send1,
    sib_send2,
    sib_recv1,
    sib_recv2,
    x_send1,
    x_send2,
    x_recv1,
    x_recv2,
    z_send1,
    z_send2,
    up_recv1,
    up_recv2,
    dn_recv1,
    dn_recv2,
    kept,
    rebuilt_ref,
    w_sem,
    g_recv1,
    g_recv2,
    g_send1,
    g_send2,
    r_recv1,
    r_recv2,
    r_send1,
    r_send2,
):
    me = lax.axis_index("latent")
    z = me // 4
    x = (me // 2) % 2
    c = me % 2
    D = res_ref.shape[1]
    wide = chunk_of(D)
    plane = 4 * rows

    def place(pz, px, pc):
        return pz * 4 + px * 2 + pc

    def block(ref, index):
        return ref.at[pl.ds(pl.multiple_of(index * rows, rows), rows)]

    weights = [
        pltpu.make_async_copy(src, dst, w_sem.at[i])
        for i, (src, dst) in enumerate(
            [(enc_hbm, enc_w), (dec_hbm, dec_w), (gate_hbm, gate_w), (up_hbm, up_w), (down_hbm, down_w)]
        )
    ]
    for copy in weights:
        copy.start()

    has_up = z < Z - 1
    has_dn = z > 0
    barrier = pltpu.get_barrier_semaphore()

    def greet(index):
        pl.semaphore_signal(barrier, inc=1, device_id={"latent": index}, device_id_type=MESH)

    greet(place(z, x, 1 - c))
    greet(place(z, 1 - x, c))

    @pl.when(has_up)
    def _():
        greet(place(z + 1, x, c))

    @pl.when(has_dn)
    def _():
        greet(place(z - 1, x, c))

    pl.semaphore_wait(barrier, 2 + (z + Z - 1) // Z + (2 * Z - 2 - z) // Z)

    def send(src, dst, send_sem, recv_sem, index):
        return pltpu.make_async_remote_copy(
            src_ref=src,
            dst_ref=dst,
            send_sem=send_sem,
            recv_sem=recv_sem,
            device_id={"latent": index},
            device_id_type=MESH,
        )

    class Gather:
        def __init__(self, buf, send_sems, recv_sems):
            self.buf, self.send_sems, self.recv_sems = buf, send_sems, recv_sems

        def copy(self, index, slot, target):
            ref = block(self.buf, index)
            return send(ref, ref, self.send_sems.at[slot], self.recv_sems.at[index], target)

        def to_x(self, p):
            return self.copy(place(p, x, c), p, place(z, 1 - x, c))

        def to_up(self, p):
            return self.copy(place(p, x, c), Z + p, place(z + 1, x, c))

        def to_dn(self, p):
            return self.copy(place(p, x, c), 2 * Z + p, place(z - 1, x, c))

        def to_sib(self, p, px):
            return self.copy(place(p, px, c), 3 * Z + 2 * p + px, place(z, x, 1 - c))

        def await_block(self, index):
            self.copy(index, 0, place(z, x, 1 - c)).wait_recv()

        def run(self, compute):
            self.to_x(z).start()

            @pl.when(has_up)
            def _():
                self.to_up(z).start()

            @pl.when(has_dn)
            def _():
                self.to_dn(z).start()

            self.to_sib(z, x).start()

            @pl.loop(0, Z + 1)
            def _(d):
                below = z - d
                above = z + d

                @pl.when((d > 0) & (below >= 0))
                def _():
                    self.await_block(place(below, x, c))
                    self.to_x(below).start()

                    @pl.when(has_up)
                    def _():
                        self.to_up(below).start()

                    self.to_sib(below, x).start()

                @pl.when((d > 0) & (above < Z))
                def _():
                    self.await_block(place(above, x, c))
                    self.to_x(above).start()

                    @pl.when(has_dn)
                    def _():
                        self.to_dn(above).start()

                    self.to_sib(above, x).start()

                @pl.loop(0, 2)
                def _(side):
                    p = z + (2 * side - 1) * (d - 1)

                    @pl.when((d > 0) & (p >= 0) & (p < Z) & (d + 1 - side > 1))
                    def _():
                        self.await_block(place(p, 1 - x, c))
                        self.to_sib(p, 1 - x).start()
                        self.await_block(place(p, x, 1 - c))
                        self.await_block(place(p, 1 - x, 1 - c))
                        compute(p)

        def drain(self):
            for p in range(Z):
                self.to_x(p).wait_send()
                self.to_sib(p, 0).wait_send()
                self.to_sib(p, 1).wait_send()

                @pl.when(has_up & (p <= z))
                def _():
                    self.to_up(p).wait_send()

                @pl.when(has_dn & (p >= z))
                def _():
                    self.to_dn(p).wait_send()

    class Scatter:
        def __init__(self, sib_send, sib_recv, x_send, x_recv, z_send, up_recv, dn_recv, send_sems, recv_sems):
            self.sib_send, self.sib_recv = sib_send, sib_recv
            self.x_send, self.x_recv = x_send, x_recv
            self.z_send, self.up_recv, self.dn_recv = z_send, up_recv, dn_recv
            self.send_sems, self.recv_sems = send_sems, recv_sems

        def copy(self, src, dst, kind, p, target):
            return send(src.at[p], dst.at[p], self.send_sems.at[kind * Z + p], self.recv_sems.at[kind * Z + p], target)

        def to_sib(self, p):
            return self.copy(self.sib_send, self.sib_recv, 0, p, place(z, x, 1 - c))

        def to_x(self, p):
            return self.copy(self.x_send, self.x_recv, 1, p, place(z, 1 - x, c))

        def to_up(self, p):
            return self.copy(self.z_send, self.up_recv, 2, p, place(z + 1, x, c))

        def to_dn(self, p):
            return self.copy(self.z_send, self.dn_recv, 3, p, place(z - 1, x, c))

        def project(self, p, acts, weight):
            blocks = [acts[i * rows : (i + 1) * rows] for i in range(4)]
            first = c == 0
            lhs = jnp.concatenate(
                [
                    jnp.where(first, blocks[1], blocks[0]),
                    jnp.where(first, blocks[3], blocks[2]),
                    jnp.where(first, blocks[0], blocks[1]),
                    jnp.where(first, blocks[2], blocks[3]),
                ],
                axis=0,
            ).astype(bf16)

            @pl.loop(0, D // wide)
            def _(k):
                cols = pl.ds(pl.multiple_of(k * wide, wide), wide)
                term = jnp.dot(lhs, weight[:, cols], preferred_element_type=f32)
                for i in range(2):
                    self.sib_send[p, i, :, cols] = term[i * rows : (i + 1) * rows].astype(bf16)
                    own_part[p, i, :, cols] = term[(2 + i) * rows : (3 + i) * rows]

            self.to_sib(p).start()

        def run(self):
            @pl.loop(0, 2 * Z)
            def _(i):
                d = Z - 1 - i // 2
                p = z + (2 * (i % 2) - 1) * d

                @pl.when((p >= 0) & (p < Z) & (d + 1 - i % 2 > 0))
                def _():
                    self.to_sib(p).wait_recv()
                    self.x_send[p] = (
                        own_part[p, 1 - x] + self.sib_recv[p, 1 - x].astype(f32)
                    ).astype(bf16)
                    self.to_x(p).start()
                    kept[p] = own_part[p, x] + self.sib_recv[p, x].astype(f32)

            @pl.loop(0, 2 * Z - 2)
            def _(i):
                d = Z - 1 - i // 2
                p = z + (2 * (i % 2) - 1) * d

                @pl.when((p >= 0) & (p < z))
                def _():
                    self.to_x(p).wait_recv()

                    @pl.when(has_up)
                    def _():
                        self.to_dn(p).wait_recv()
                        self.z_send[p] = (
                            kept[p] + self.x_recv[p].astype(f32) + self.dn_recv[p].astype(f32)
                        ).astype(bf16)

                    @pl.when(z == Z - 1)
                    def _():
                        self.z_send[p] = (kept[p] + self.x_recv[p].astype(f32)).astype(bf16)

                    self.to_dn(p).start()

                @pl.when((p > z) & (p < Z))
                def _():
                    self.to_x(p).wait_recv()

                    @pl.when(has_dn)
                    def _():
                        self.to_up(p).wait_recv()
                        self.z_send[p] = (
                            kept[p] + self.x_recv[p].astype(f32) + self.up_recv[p].astype(f32)
                        ).astype(bf16)

                    @pl.when(z == 0)
                    def _():
                        self.z_send[p] = (kept[p] + self.x_recv[p].astype(f32)).astype(bf16)

                    self.to_up(p).start()

            self.to_x(z).wait_recv()
            kept[z] += self.x_recv[z].astype(f32)

            @pl.when(has_up)
            def _():
                self.to_dn(z).wait_recv()
                kept[z] += self.dn_recv[z].astype(f32)

            @pl.when(has_dn)
            def _():
                self.to_up(z).wait_recv()
                kept[z] += self.up_recv[z].astype(f32)

            return kept[z]

        def drain(self):
            for p in range(Z):
                self.to_sib(p).wait_send()
                self.to_x(p).wait_send()

                @pl.when(p > z)
                def _():
                    self.to_up(p).wait_send()

                @pl.when(p < z)
                def _():
                    self.to_dn(p).wait_send()

    gather1 = Gather(gath1, g_send1, g_recv1)
    gather2 = Gather(gath2, g_send2, g_recv2)
    scatter1 = Scatter(
        sib_send1, sib_recv1, x_send1, x_recv1, z_send1, up_recv1, dn_recv1, r_send1, r_recv1
    )
    scatter2 = Scatter(
        sib_send2, sib_recv2, x_send2, x_recv2, z_send2, up_recv2, dn_recv2, r_send2, r_recv2
    )

    def product(buf, p, mats):
        lhs_rows = pl.ds(pl.multiple_of(p * plane, plane), plane)

        def step(k, sums):
            part = pl.ds(pl.multiple_of(k * wide, wide), wide)
            lhs = buf[lhs_rows, part]
            return tuple(
                total + jnp.dot(lhs, mat[part, :], preferred_element_type=f32)
                for total, mat in zip(sums, mats)
            )

        zeros = tuple(jnp.zeros((plane, mat.shape[1]), f32) for mat in mats)
        return lax.fori_loop(0, D // wide, step, zeros)

    def encode(p):
        (total,) = product(gath1, p, (enc_w,))
        preact = total + bias_ref[...]
        acts = preact * jax.nn.sigmoid(sharpness * (preact - thr_ref[...]))
        scatter1.project(p, acts, dec_w)

    def feed_hidden(p):
        gate_proj, up_proj = product(gath2, p, (gate_w, up_w))
        scatter2.project(p, jax.nn.gelu(gate_proj, approximate=True) * up_proj, down_w)

    block(gath1, me)[...] = res_ref[...]
    weights[0].wait()
    weights[1].wait()
    gather1.run(encode)
    rebuilt = scatter1.run() + dec_bias_ref[...]
    rebuilt_ref[...] = rebuilt
    block(gath2, me)[...] = rms_scale(rebuilt, pre_gain_ref[...]).astype(bf16)
    weights[2].wait()
    weights[3].wait()
    weights[4].wait()
    gather2.run(feed_hidden)
    ffn_sum = scatter2.run()
    out_ref[...] = (rebuilt_ref[...] + rms_scale(ffn_sum, post_gain_ref[...])).astype(bf16)
    for phase in (gather1, scatter1, gather2, scatter2):
        phase.drain()


def fused_device(
    n,
    residual,
    enc_weight,
    enc_bias,
    threshold,
    dec_weight,
    dec_bias,
    pre_gain,
    gate_weight,
    up_weight,
    down_weight,
    post_gain,
):
    rows, D = residual.shape
    Z = n // 4
    vmem = pl.BlockSpec(memory_space=pltpu.VMEM)
    hbm = pl.BlockSpec(memory_space=pl.ANY)

    def twice(shape, dtype):
        return [pltpu.VMEM(shape, dtype)] * 2

    def sems(count):
        return [pltpu.SemaphoreType.DMA((count,))] * 2

    latents, hidden = enc_weight.shape[1], gate_weight.shape[1]
    return pl.pallas_call(
        functools.partial(kernel, Z, rows),
        out_shape=jax.ShapeDtypeStruct(residual.shape, bf16),
        in_specs=[vmem, hbm, vmem, vmem, hbm, vmem, vmem, hbm, hbm, hbm, vmem],
        out_specs=vmem,
        scratch_shapes=[
            pltpu.VMEM(enc_weight.shape, bf16),
            pltpu.VMEM(dec_weight.shape, bf16),
            pltpu.VMEM(gate_weight.shape, bf16),
            pltpu.VMEM(up_weight.shape, bf16),
            pltpu.VMEM(down_weight.shape, bf16),
            *twice((n * rows, D), bf16),
            pltpu.VMEM((Z, 2, rows, D), f32),
            *twice((Z, 2, rows, D), bf16),
            *twice((Z, 2, rows, D), bf16),
            *twice((Z, rows, D), bf16),
            *twice((Z, rows, D), bf16),
            *twice((Z, rows, D), bf16),
            *twice((Z, rows, D), bf16),
            *twice((Z, rows, D), bf16),
            pltpu.VMEM((Z, rows, D), f32),
            pltpu.VMEM((rows, D), f32),
            pltpu.SemaphoreType.DMA((5,)),
            *sems(n),
            *sems(5 * Z),
            *sems(4 * Z),
            *sems(4 * Z),
        ],
        compiler_params=pltpu.CompilerParams(
            collective_id=0, has_side_effects=True, vmem_limit_bytes=52 * 1024 * 1024
        ),
        cost_estimate=pl.CostEstimate(
            flops=2 * n * rows * D * (2 * latents + 3 * hidden),
            bytes_accessed=2 * D * (2 * latents + 3 * hidden),
            transcendentals=n * rows * (latents + hidden),
        ),
    )(
        residual,
        enc_weight,
        enc_bias.reshape(1, -1),
        threshold.reshape(1, -1),
        dec_weight,
        dec_bias.reshape(1, -1),
        pre_gain.reshape(1, -1),
        gate_weight,
        up_weight,
        down_weight,
        post_gain.reshape(1, -1),
    )


def solution(mesh):
    n = mesh.shape["latent"]

    def per_device(residual, *rest):
        rows, width = residual.shape
        if n % 4 == 0 and rows % 16 == 0 and width % 128 == 0:
            return fused_device(n, residual, *rest)
        return plain_device(residual, *rest)

    return jax.shard_map(
        per_device,
        mesh=mesh,
        in_specs=(
            P(("parts", "latent"), None),
            P(None, "latent"),
            P("latent"),
            P("latent"),
            P("latent", None),
            P(),
            P(),
            P(None, "latent"),
            P(None, "latent"),
            P("latent", None),
            P(),
        ),
        out_specs=P(("parts", "latent"), None),
        check_vma=False,
    )
```

```python
import functools

import jax
import jax.numpy as jnp
from jax import lax
from jax.experimental import pallas as pl
from jax.experimental.pallas import tpu as pltpu
from jax.sharding import PartitionSpec as P

sharpness = 10.0
epsilon = 1e-06
MESH = pl.DeviceIdType.MESH
f32 = jnp.float32
bf16 = jnp.bfloat16


def rms_scale(values, gain):
    return values * lax.rsqrt(jnp.mean(values * values, axis=-1, keepdims=True) + epsilon) * gain


def plain_device(
    residual,
    enc_weight,
    enc_bias,
    threshold,
    dec_weight,
    dec_bias,
    pre_gain,
    gate_weight,
    up_weight,
    down_weight,
    post_gain,
):
    def encode(block_rows):
        preact = jnp.dot(block_rows, enc_weight, preferred_element_type=f32) + enc_bias
        return (preact * jax.nn.sigmoid(sharpness * (preact - threshold))).astype(bf16)

    def feed_hidden(block_rows):
        gate_proj = jnp.dot(block_rows, gate_weight, preferred_element_type=f32)
        up_proj = jnp.dot(block_rows, up_weight, preferred_element_type=f32)
        return (jax.nn.gelu(gate_proj, approximate=True) * up_proj).astype(bf16)

    def scatter_sum(lhs, rhs):
        return lax.psum_scatter(
            jnp.dot(lhs, rhs, preferred_element_type=f32), "latent", scatter_dimension=0, tiled=True
        )

    latent_acts = encode(lax.all_gather(residual, "latent", axis=0, tiled=True))
    rebuilt = scatter_sum(latent_acts, dec_weight) + dec_bias
    normed = rms_scale(rebuilt, pre_gain).astype(bf16)
    hidden = feed_hidden(lax.all_gather(normed, "latent", axis=0, tiled=True))
    ffn_sum = scatter_sum(hidden, down_weight)
    return (rebuilt + rms_scale(ffn_sum, post_gain)).astype(bf16)


def halves_of(extent):
    return 2 if extent % 256 == 0 else 1


def chunk_of(extent):
    for pieces in (6, 4, 8, 2):
        if extent % (128 * pieces) == 0:
            return extent // pieces
    return extent


def kernel(
    Z,
    rows,
    res_ref,
    enc_hbm,
    bias_ref,
    thr_ref,
    dec_hbm,
    dec_bias_ref,
    pre_gain_ref,
    gate_hbm,
    up_hbm,
    down_hbm,
    post_gain_ref,
    out_ref,
    enc_w,
    dec_w,
    gate_w,
    up_w,
    down_w,
    gath1,
    gath2,
    own_part,
    sib_send1,
    sib_send2,
    sib_recv1,
    sib_recv2,
    x_send1,
    x_send2,
    x_recv1,
    x_recv2,
    z_send1,
    z_send2,
    up_recv1,
    up_recv2,
    dn_recv1,
    dn_recv2,
    kept,
    rebuilt_ref,
    w_sem,
    g_recv1,
    g_recv2,
    g_send1,
    g_send2,
    r_recv1,
    r_recv2,
    r_send1,
    r_send2,
):
    me = lax.axis_index("latent")
    z = me // 4
    x = (me // 2) % 2
    c = me % 2
    D = res_ref.shape[1]
    wide = chunk_of(D)
    halves = halves_of(D)
    half = D // halves
    plane = 4 * rows

    def place(pz, px, pc):
        return pz * 4 + px * 2 + pc

    arrival = [sorted(range(Z), key=lambda p: (abs(p - own), p)) for own in range(Z)]
    leaving = [[order[-2], order[-1], *order[-3::-1]] for order in arrival]

    def pick(table, k):
        value = 0
        for own in range(Z):
            for place_in_order in range(Z):
                value += jnp.where((z == own) & (k == place_in_order), table[own][place_in_order], 0)
        return value

    def block(ref, index):
        return ref.at[pl.ds(pl.multiple_of(index * rows, rows), rows)]

    weights = [
        pltpu.make_async_copy(src, dst, w_sem.at[i])
        for i, (src, dst) in enumerate(
            [(enc_hbm, enc_w), (dec_hbm, dec_w), (gate_hbm, gate_w), (up_hbm, up_w), (down_hbm, down_w)]
        )
    ]
    weights[0].start()
    weights[1].start()

    has_up = z < Z - 1
    has_dn = z > 0
    barrier = pltpu.get_barrier_semaphore()

    def greet(index):
        pl.semaphore_signal(barrier, inc=1, device_id={"latent": index}, device_id_type=MESH)

    greet(place(z, x, 1 - c))
    greet(place(z, 1 - x, c))

    @pl.when(has_up)
    def _():
        greet(place(z + 1, x, c))

    @pl.when(has_dn)
    def _():
        greet(place(z - 1, x, c))

    pl.semaphore_wait(barrier, 2 + (z + Z - 1) // Z + (2 * Z - 2 - z) // Z)

    def send(src, dst, send_sem, recv_sem, index):
        return pltpu.make_async_remote_copy(
            src_ref=src,
            dst_ref=dst,
            send_sem=send_sem,
            recv_sem=recv_sem,
            device_id={"latent": index},
            device_id_type=MESH,
        )

    class Gather:
        def __init__(self, buf, send_sems, recv_sems):
            self.buf, self.send_sems, self.recv_sems = buf, send_sems, recv_sems

        def copy(self, index, slot, target):
            ref = block(self.buf, index)
            return send(ref, ref, self.send_sems.at[slot], self.recv_sems.at[index], target)

        def to_x(self, p):
            return self.copy(place(p, x, c), p, place(z, 1 - x, c))

        def to_up(self, p):
            return self.copy(place(p, x, c), Z + p, place(z + 1, x, c))

        def to_dn(self, p):
            return self.copy(place(p, x, c), 2 * Z + p, place(z - 1, x, c))

        def to_sib(self, p, px):
            return self.copy(place(p, px, c), 3 * Z + 2 * p + px, place(z, x, 1 - c))

        def await_block(self, index):
            self.copy(index, 0, place(z, x, 1 - c)).wait_recv()

        def run(self, compute, before_last):
            self.to_x(z).start()

            @pl.when(has_up)
            def _():
                self.to_up(z).start()

            @pl.when(has_dn)
            def _():
                self.to_dn(z).start()

            self.to_sib(z, x).start()

            @pl.loop(0, Z + 1)
            def _(d):
                below = z - d
                above = z + d

                @pl.when((d > 0) & (below >= 0))
                def _():
                    self.await_block(place(below, x, c))
                    self.to_x(below).start()

                    @pl.when(has_up)
                    def _():
                        self.to_up(below).start()

                    self.to_sib(below, x).start()

                @pl.when((d > 0) & (above < Z))
                def _():
                    self.await_block(place(above, x, c))
                    self.to_x(above).start()

                    @pl.when(has_dn)
                    def _():
                        self.to_dn(above).start()

                    self.to_sib(above, x).start()

                @pl.loop(0, 2)
                def _(side):
                    p = z + (2 * side - 1) * (d - 1)

                    @pl.when((d > 0) & (p >= 0) & (p < Z) & (d + 1 - side > 1))
                    def _():
                        self.await_block(place(p, 1 - x, c))
                        self.to_sib(p, 1 - x).start()
                        self.await_block(place(p, x, 1 - c))
                        self.await_block(place(p, 1 - x, 1 - c))

                        @pl.when(p == pick(arrival, Z - 1))
                        def _():
                            before_last()

                        compute(p)

        def drain(self):
            for p in range(Z):
                self.to_x(p).wait_send()
                self.to_sib(p, 0).wait_send()
                self.to_sib(p, 1).wait_send()

                @pl.when(has_up & (p <= z))
                def _():
                    self.to_up(p).wait_send()

                @pl.when(has_dn & (p >= z))
                def _():
                    self.to_dn(p).wait_send()

    class Scatter:
        def __init__(self, sib_send, sib_recv, x_send, x_recv, z_send, up_recv, dn_recv, send_sems, recv_sems):
            self.sib_send, self.sib_recv = sib_send, sib_recv
            self.x_send, self.x_recv = x_send, x_recv
            self.z_send, self.up_recv, self.dn_recv = z_send, up_recv, dn_recv
            self.send_sems, self.recv_sems = send_sems, recv_sems

        def copy(self, src, dst, kind, p, h, target):
            cols = pl.ds(pl.multiple_of(h * half, half), half)
            slot = kind * Z * halves + p * halves + h
            return send(
                src.at[p, :, cols], dst.at[p, :, cols], self.send_sems.at[slot], self.recv_sems.at[slot], target
            )

        def to_sib(self, p):
            return send(
                self.sib_send.at[p], self.sib_recv.at[p], self.send_sems.at[p], self.recv_sems.at[p], place(z, x, 1 - c)
            )

        def to_x(self, p, h):
            return self.copy(self.x_send, self.x_recv, 1, p, h, place(z, 1 - x, c))

        def to_up(self, p, h):
            return self.copy(self.z_send, self.up_recv, 2, p, h, place(z + 1, x, c))

        def to_dn(self, p, h):
            return self.copy(self.z_send, self.dn_recv, 3, p, h, place(z - 1, x, c))

        def project(self, p, acts, weight):
            blocks = [acts[i * rows : (i + 1) * rows] for i in range(4)]
            first = c == 0
            lhs = jnp.concatenate(
                [
                    jnp.where(first, blocks[1], blocks[0]),
                    jnp.where(first, blocks[3], blocks[2]),
                    jnp.where(first, blocks[0], blocks[1]),
                    jnp.where(first, blocks[2], blocks[3]),
                ],
                axis=0,
            ).astype(bf16)

            @pl.loop(0, D // wide)
            def _(k):
                cols = pl.ds(pl.multiple_of(k * wide, wide), wide)
                term = jnp.dot(lhs, weight[:, cols], preferred_element_type=f32)
                for i in range(2):
                    self.sib_send[p, i, :, cols] = term[i * rows : (i + 1) * rows].astype(bf16)
                    own_part[p, i, :, cols] = term[(2 + i) * rows : (3 + i) * rows]

            self.to_sib(p).start()

        def start_x(self, j):
            p, h = pick(leaving, j // halves), j % halves
            cols = pl.ds(pl.multiple_of(h * half, half), half)

            @pl.when(h == 0)
            def _():
                self.to_sib(p).wait_recv()

            self.x_send[p, :, cols] = (
                own_part[p, 1 - x, :, cols] + self.sib_recv[p, 1 - x, :, cols].astype(f32)
            ).astype(bf16)
            self.to_x(p, h).start()
            kept[p, :, cols] = own_part[p, x, :, cols] + self.sib_recv[p, x, :, cols].astype(f32)

        def start_first(self):
            for j in range(halves):
                self.start_x(j)

        def run(self):
            @pl.loop(0, Z * halves)
            def _(j):
                p, h = pick(leaving, j // halves), j % halves
                cols = pl.ds(pl.multiple_of(h * half, half), half)
                self.to_x(p, h).wait_send()

                @pl.when(j + halves < Z * halves)
                def _():
                    self.start_x(j + halves)

                self.to_x(p, h).wait_recv()
                kept[p, :, cols] += self.x_recv[p, :, cols].astype(f32)

                @pl.when((p <= z) & has_up)
                def _():
                    self.to_dn(p, h).wait_recv()
                    kept[p, :, cols] += self.dn_recv[p, :, cols].astype(f32)

                @pl.when((p >= z) & has_dn)
                def _():
                    self.to_up(p, h).wait_recv()
                    kept[p, :, cols] += self.up_recv[p, :, cols].astype(f32)

                @pl.when(p != z)
                def _():
                    self.z_send[p, :, cols] = kept[p, :, cols].astype(bf16)

                @pl.when(p < z)
                def _():
                    self.to_dn(p, h).start()

                @pl.when(p > z)
                def _():
                    self.to_up(p, h).start()

            return kept[z]

        def drain(self):
            for p in range(Z):
                self.to_sib(p).wait_send()
                for h in range(halves):

                    @pl.when(p > z)
                    def _():
                        self.to_up(p, h).wait_send()

                    @pl.when(p < z)
                    def _():
                        self.to_dn(p, h).wait_send()

    gather1 = Gather(gath1, g_send1, g_recv1)
    gather2 = Gather(gath2, g_send2, g_recv2)
    scatter1 = Scatter(
        sib_send1, sib_recv1, x_send1, x_recv1, z_send1, up_recv1, dn_recv1, r_send1, r_recv1
    )
    scatter2 = Scatter(
        sib_send2, sib_recv2, x_send2, x_recv2, z_send2, up_recv2, dn_recv2, r_send2, r_recv2
    )

    def lhs_of(buf, p, k):
        return buf[pl.ds(pl.multiple_of(p * plane, plane), plane), part_of(k)]

    def part_of(k):
        return pl.ds(pl.multiple_of(k * wide, wide), wide)

    def encode(p):
        @pl.when(p == z)
        def _():
            weights[0].wait()
            weights[1].wait()
            for copy in weights[2:]:
                copy.start()

        def step(k, total):
            return total + jnp.dot(lhs_of(gath1, p, k), enc_w[part_of(k), :], preferred_element_type=f32)

        total = lax.fori_loop(0, D // wide, step, jnp.zeros((plane, enc_w.shape[1]), f32))
        preact = total + bias_ref[...].reshape(1, -1)
        acts = preact * jax.nn.sigmoid(sharpness * (preact - thr_ref[...].reshape(1, -1)))
        scatter1.project(p, acts, dec_w)

    def feed_hidden(p):
        def step(k, totals):
            lhs = lhs_of(gath2, p, k)
            return tuple(
                total
                + lax.dot_general(lhs, mat[:, part_of(k)], (((1,), (1,)), ((), ())), preferred_element_type=f32)
                for total, mat in zip(totals, (gate_w, up_w))
            )

        zeros = jnp.zeros((plane, gate_w.shape[0]), f32)
        gate_proj, up_proj = lax.fori_loop(0, D // wide, step, (zeros, zeros))
        scatter2.project(p, jax.nn.gelu(gate_proj, approximate=True) * up_proj, down_w)

    block(gath1, me)[...] = res_ref[...]
    gather1.run(encode, scatter1.start_first)
    rebuilt = scatter1.run() + dec_bias_ref[...].reshape(1, -1)
    rebuilt_ref[...] = rebuilt
    block(gath2, me)[...] = rms_scale(rebuilt, pre_gain_ref[...].reshape(1, -1)).astype(bf16)
    for copy in weights[2:]:
        copy.wait()
    gather2.run(feed_hidden, scatter2.start_first)
    ffn_sum = scatter2.run()
    out_ref[...] = (rebuilt_ref[...] + rms_scale(ffn_sum, post_gain_ref[...].reshape(1, -1))).astype(bf16)
    for phase in (gather1, scatter1, gather2, scatter2):
        phase.drain()


def fused_device(
    n,
    residual,
    enc_weight,
    enc_bias,
    threshold,
    dec_weight,
    dec_bias,
    pre_gain,
    gate_weight,
    up_weight,
    down_weight,
    post_gain,
):
    rows, D = residual.shape
    Z = n // 4
    vmem = pl.BlockSpec(memory_space=pltpu.VMEM)
    hbm = pl.BlockSpec(memory_space=pl.ANY)

    def twice(shape, dtype):
        return [pltpu.VMEM(shape, dtype)] * 2

    def sems(count):
        return [pltpu.SemaphoreType.DMA((count,))] * 2

    latents, hidden = enc_weight.shape[1], gate_weight.shape[1]
    return pl.pallas_call(
        functools.partial(kernel, Z, rows),
        out_shape=jax.ShapeDtypeStruct(residual.shape, bf16),
        in_specs=[vmem, hbm, vmem, vmem, hbm, vmem, vmem, hbm, hbm, hbm, vmem],
        out_specs=vmem,
        scratch_shapes=[
            pltpu.VMEM(enc_weight.shape, bf16),
            pltpu.VMEM(dec_weight.shape, bf16),
            pltpu.VMEM(gate_weight.shape[::-1], bf16),
            pltpu.VMEM(up_weight.shape[::-1], bf16),
            pltpu.VMEM(down_weight.shape, bf16),
            *twice((n * rows, D), bf16),
            pltpu.VMEM((Z, 2, rows, D), f32),
            *twice((Z, 2, rows, D), bf16),
            *twice((Z, 2, rows, D), bf16),
            *twice((Z, rows, D), bf16),
            *twice((Z, rows, D), bf16),
            *twice((Z, rows, D), bf16),
            *twice((Z, rows, D), bf16),
            *twice((Z, rows, D), bf16),
            pltpu.VMEM((Z, rows, D), f32),
            pltpu.VMEM((rows, D), f32),
            pltpu.SemaphoreType.DMA((5,)),
            *sems(n),
            *sems(5 * Z),
            *sems(4 * Z * halves_of(D)),
            *sems(4 * Z * halves_of(D)),
        ],
        compiler_params=pltpu.CompilerParams(
            collective_id=0, has_side_effects=True, vmem_limit_bytes=60 * 1024 * 1024
        ),
        cost_estimate=pl.CostEstimate(
            flops=2 * n * rows * D * (2 * latents + 3 * hidden),
            bytes_accessed=2 * D * (2 * latents + 3 * hidden),
            transcendentals=n * rows * (latents + hidden),
        ),
    )(
        residual,
        enc_weight,
        enc_bias,
        threshold,
        dec_weight,
        dec_bias,
        pre_gain,
        gate_weight.T,
        up_weight.T,
        down_weight,
        post_gain,
    )


def solution(mesh):
    n = mesh.shape["latent"]

    def per_device(residual, *rest):
        rows, width = residual.shape
        if n % 4 == 0 and rows % 16 == 0 and width % 128 == 0:
            return fused_device(n, residual, *rest)
        return plain_device(residual, *rest)

    return jax.shard_map(
        per_device,
        mesh=mesh,
        in_specs=(
            P(("parts", "latent"), None),
            P(None, "latent"),
            P("latent"),
            P("latent"),
            P("latent", None),
            P(),
            P(),
            P(None, "latent"),
            P(None, "latent"),
            P("latent", None),
            P(),
        ),
        out_specs=P(("parts", "latent"), None),
        check_vma=False,
    )
```

```python
import functools

import jax
import jax.numpy as jnp
from jax import lax
from jax.experimental import pallas as pl
from jax.experimental.pallas import tpu as pltpu
from jax.sharding import PartitionSpec as P

sharpness = 10.0
epsilon = 1e-06
MESH = pl.DeviceIdType.MESH
f32 = jnp.float32
bf16 = jnp.bfloat16


def rms_scale(values, gain):
    return values * lax.rsqrt(jnp.mean(values * values, axis=-1, keepdims=True) + epsilon) * gain


def plain_device(
    residual,
    enc_weight,
    enc_bias,
    threshold,
    dec_weight,
    dec_bias,
    pre_gain,
    gate_weight,
    up_weight,
    down_weight,
    post_gain,
):
    def encode(block_rows):
        preact = jnp.dot(block_rows, enc_weight, preferred_element_type=f32) + enc_bias
        return (preact * jax.nn.sigmoid(sharpness * (preact - threshold))).astype(bf16)

    def feed_hidden(block_rows):
        gate_proj = jnp.dot(block_rows, gate_weight, preferred_element_type=f32)
        up_proj = jnp.dot(block_rows, up_weight, preferred_element_type=f32)
        return (jax.nn.gelu(gate_proj, approximate=True) * up_proj).astype(bf16)

    def scatter_sum(lhs, rhs):
        return lax.psum_scatter(
            jnp.dot(lhs, rhs, preferred_element_type=f32), "latent", scatter_dimension=0, tiled=True
        )

    latent_acts = encode(lax.all_gather(residual, "latent", axis=0, tiled=True))
    rebuilt = scatter_sum(latent_acts, dec_weight) + dec_bias
    normed = rms_scale(rebuilt, pre_gain).astype(bf16)
    hidden = feed_hidden(lax.all_gather(normed, "latent", axis=0, tiled=True))
    ffn_sum = scatter_sum(hidden, down_weight)
    return (rebuilt + rms_scale(ffn_sum, post_gain)).astype(bf16)


def halves_of(extent):
    return 2 if extent % 256 == 0 else 1


def chunk_of(extent):
    for pieces in (6, 4, 8, 2):
        if extent % (128 * pieces) == 0:
            return extent // pieces
    return extent


def kernel(
    Z,
    rows,
    res_ref,
    enc_hbm,
    bias_ref,
    thr_ref,
    dec_hbm,
    dec_bias_ref,
    pre_gain_ref,
    gate_hbm,
    up_hbm,
    down_hbm,
    post_gain_ref,
    out_ref,
    enc_w,
    dec_w,
    gate_w,
    up_w,
    down_w,
    gath1,
    gath2,
    own_part,
    sib_send1,
    sib_send2,
    sib_recv1,
    sib_recv2,
    x_send1,
    x_send2,
    x_recv1,
    x_recv2,
    z_send1,
    z_send2,
    up_recv1,
    up_recv2,
    dn_recv1,
    dn_recv2,
    kept,
    rebuilt_ref,
    w_sem,
    g_recv1,
    g_recv2,
    g_send1,
    g_send2,
    r_recv1,
    r_recv2,
    r_send1,
    r_send2,
):
    me = lax.axis_index("latent")
    z = me // 4
    x = (me // 2) % 2
    c = me % 2
    D = res_ref.shape[1]
    wide = chunk_of(D)
    halves = halves_of(D)
    half = D // halves
    plane = 4 * rows

    def place(pz, px, pc):
        return pz * 4 + px * 2 + pc

    def order_of(own):
        step = 1 - 2 * (own % 2)
        planes = [own] + [own + side * step * d for d in range(1, Z) for side in (1, -1)]
        return [p for p in planes if 0 <= p < Z]

    arrival = [order_of(own) for own in range(Z)]
    leaving = [[order[1], *order[:1:-1], order[0]] for order in arrival]
    passing = [[order[-1], order[1], *order[-2:1:-1], order[0]] for order in arrival]
    groups = [sorted(range(Z // 2), key=lambda g: (abs(g - own // 2), g)) for own in range(Z)]

    def pick(table, k):
        value = 0
        for own in range(Z):
            for place_in_order in range(len(table[own])):
                value += jnp.where((z == own) & (k == place_in_order), table[own][place_in_order], 0)
        return value

    def block(ref, index):
        return ref.at[pl.ds(pl.multiple_of(index * rows, rows), rows)]

    weights = [
        pltpu.make_async_copy(src, dst, w_sem.at[i])
        for i, (src, dst) in enumerate(
            [(enc_hbm, enc_w), (dec_hbm, dec_w), (gate_hbm, gate_w), (up_hbm, up_w), (down_hbm, down_w)]
        )
    ]
    weights[0].start()
    weights[1].start()

    has_up = z < Z - 1
    has_dn = z > 0
    barrier = pltpu.get_barrier_semaphore()

    def greet(index):
        pl.semaphore_signal(barrier, inc=1, device_id={"latent": index}, device_id_type=MESH)

    greet(place(z, x, 1 - c))
    greet(place(z, 1 - x, c))

    @pl.when(has_up)
    def _():
        greet(place(z + 1, x, c))

    @pl.when(has_dn)
    def _():
        greet(place(z - 1, x, c))

    pl.semaphore_wait(barrier, 2 + (z + Z - 1) // Z + (2 * Z - 2 - z) // Z)

    def send(src, dst, send_sem, recv_sem, index):
        return pltpu.make_async_remote_copy(
            src_ref=src,
            dst_ref=dst,
            send_sem=send_sem,
            recv_sem=recv_sem,
            device_id={"latent": index},
            device_id_type=MESH,
        )

    class Gather:
        def __init__(self, buf, send_sems, recv_sems):
            self.buf, self.send_sems, self.recv_sems = buf, send_sems, recv_sems

        def copy(self, index, slot, target):
            ref = block(self.buf, index)
            return send(ref, ref, self.send_sems.at[slot], self.recv_sems.at[index], target)

        def to_x(self, p):
            return self.copy(place(p, x, c), p, place(z, 1 - x, c))

        def to_up(self, p):
            return self.copy(place(p, x, c), Z + p, place(z + 1, x, c))

        def to_dn(self, p):
            return self.copy(place(p, x, c), 2 * Z + p, place(z - 1, x, c))

        def to_sib(self, p, px):
            return self.copy(place(p, px, c), 3 * Z + 2 * p + px, place(z, x, 1 - c))

        def await_block(self, index):
            self.copy(index, 0, place(z, x, 1 - c)).wait_recv()

        def run(self, compute, before_last):
            self.to_x(z).start()

            @pl.when(has_up)
            def _():
                self.to_up(z).start()

            @pl.when(has_dn)
            def _():
                self.to_dn(z).start()

            self.to_sib(z, x).start()
            toward = 1 - 2 * (z % 2)

            for d in range(1, Z):
                first, second = z + toward * d, z - toward * d
                first_is = (first >= 0) & (first < Z)

                @pl.when(first_is)
                def _():
                    self.pass_on(first)
                    self.to_x(first).start()

                @pl.when((second >= 0) & (second < Z))
                def _():
                    self.pass_on(second)

                    @pl.when(first_is)
                    def _():
                        self.to_x(first).wait_send()

                    self.to_x(second).start()

            @pl.loop(0, Z // 2)
            def _(g):
                for k in range(Z):

                    @pl.when(g == (0 if k < 2 else 1))
                    def _():
                        p = pick(arrival, k)
                        self.await_block(place(p, 1 - x, c))
                        self.to_sib(p, 1 - x).start()

                group = pick(groups, g)
                for p in (2 * group, 2 * group + 1):
                    for px in range(2):
                        self.await_block(place(p, px, 1 - c))

                @pl.when(g == Z // 2 - 1)
                def _():
                    before_last()

                compute(group)

        def pass_on(self, p):
            self.await_block(place(p, x, c))

            @pl.when((p < z) & has_up)
            def _():
                self.to_up(p).start()

            @pl.when((p > z) & has_dn)
            def _():
                self.to_dn(p).start()

            self.to_sib(p, x).start()

        def drain(self):
            toward = 1 - 2 * (z % 2)
            for p in range(Z):
                mirror = 2 * z - p

                @pl.when(((p - z) * toward <= 0) | (mirror < 0) | (mirror >= Z))
                def _():
                    self.to_x(p).wait_send()

                self.to_sib(p, 0).wait_send()
                self.to_sib(p, 1).wait_send()

                @pl.when(has_up & (p <= z))
                def _():
                    self.to_up(p).wait_send()

                @pl.when(has_dn & (p >= z))
                def _():
                    self.to_dn(p).wait_send()

    class Scatter:
        def __init__(self, sib_send, sib_recv, x_send, x_recv, z_send, up_recv, dn_recv, send_sems, recv_sems):
            self.sib_send, self.sib_recv = sib_send, sib_recv
            self.x_send, self.x_recv = x_send, x_recv
            self.z_send, self.up_recv, self.dn_recv = z_send, up_recv, dn_recv
            self.send_sems, self.recv_sems = send_sems, recv_sems

        def copy(self, src, dst, kind, p, h, target):
            cols = pl.ds(pl.multiple_of(h * half, half), half)
            slot = kind * Z * halves + p * halves + h
            return send(
                src.at[p, :, cols], dst.at[p, :, cols], self.send_sems.at[slot], self.recv_sems.at[slot], target
            )

        def to_sib(self, p):
            return send(
                self.sib_send.at[p], self.sib_recv.at[p], self.send_sems.at[p], self.recv_sems.at[p], place(z, x, 1 - c)
            )

        def to_x(self, p, h):
            return self.copy(self.x_send, self.x_recv, 1, p, h, place(z, 1 - x, c))

        def to_up(self, p, h):
            return self.copy(self.z_send, self.up_recv, 2, p, h, place(z + 1, x, c))

        def to_dn(self, p, h):
            return self.copy(self.z_send, self.dn_recv, 3, p, h, place(z - 1, x, c))

        def project(self, group, acts, weight):
            blocks = [acts[i * rows : (i + 1) * rows] for i in range(8)]
            first = c == 0
            others = [jnp.where(first, blocks[i + 1], blocks[i]) for i in range(0, 8, 2)]
            own = [jnp.where(first, blocks[i], blocks[i + 1]) for i in range(0, 8, 2)]
            lhs = jnp.concatenate(others + own, axis=0).astype(bf16)
            for k in range(D // wide):
                cols = slice(k * wide, (k + 1) * wide)
                term = jnp.dot(lhs, weight[:, cols], preferred_element_type=f32)
                for i in range(4):
                    p = 2 * group + i // 2
                    self.sib_send[p, i % 2, :, cols] = term[i * rows : (i + 1) * rows].astype(bf16)
                    own_part[p, i % 2, :, cols] = term[(4 + i) * rows : (5 + i) * rows]

            self.to_sib(2 * group).start()
            self.to_sib(2 * group + 1).start()

        def start_x(self, j):
            p, h = pick(leaving, j // halves), j % halves
            cols = pl.ds(pl.multiple_of(h * half, half), half)

            @pl.when(h == 0)
            def _():
                self.to_sib(p).wait_recv()

            self.x_send[p, :, cols] = (
                own_part[p, 1 - x, :, cols] + self.sib_recv[p, 1 - x, :, cols].astype(f32)
            ).astype(bf16)
            self.to_x(p, h).start()
            kept[p, :, cols] = own_part[p, x, :, cols] + self.sib_recv[p, x, :, cols].astype(f32)

        def start_first(self):
            for j in range(halves):
                self.start_x(j)

        def run(self):
            for j in range(halves, 2 * halves):
                self.start_x(j)

            @pl.loop(0, Z * halves)
            def _(j):
                @pl.when(j + 2 * halves < Z * halves)
                def _():
                    self.to_x(pick(leaving, j // halves + 1), j % halves).wait_send()
                    self.start_x(j + 2 * halves)

                p, h = pick(passing, j // halves), j % halves
                cols = pl.ds(pl.multiple_of(h * half, half), half)
                self.to_x(p, h).wait_recv()
                kept[p, :, cols] += self.x_recv[p, :, cols].astype(f32)

                @pl.when((p <= z) & has_up)
                def _():
                    self.to_dn(p, h).wait_recv()
                    kept[p, :, cols] += self.dn_recv[p, :, cols].astype(f32)

                @pl.when((p >= z) & has_dn)
                def _():
                    self.to_up(p, h).wait_recv()
                    kept[p, :, cols] += self.up_recv[p, :, cols].astype(f32)

                @pl.when(p != z)
                def _():
                    self.z_send[p, :, cols] = kept[p, :, cols].astype(bf16)

                @pl.when(p < z)
                def _():
                    self.to_dn(p, h).start()

                @pl.when(p > z)
                def _():
                    self.to_up(p, h).start()

            return kept[z]

        def drain(self):
            for p in range(Z):
                self.to_sib(p).wait_send()
                for h in range(halves):

                    @pl.when((p == pick(leaving, 0)) | (p == pick(leaving, Z - 1)))
                    def _():
                        self.to_x(p, h).wait_send()

                    @pl.when(p > z)
                    def _():
                        self.to_up(p, h).wait_send()

                    @pl.when(p < z)
                    def _():
                        self.to_dn(p, h).wait_send()

    gather1 = Gather(gath1, g_send1, g_recv1)
    gather2 = Gather(gath2, g_send2, g_recv2)
    scatter1 = Scatter(
        sib_send1, sib_recv1, x_send1, x_recv1, z_send1, up_recv1, dn_recv1, r_send1, r_recv1
    )
    scatter2 = Scatter(
        sib_send2, sib_recv2, x_send2, x_recv2, z_send2, up_recv2, dn_recv2, r_send2, r_recv2
    )

    def rows_of(buf, group):
        return buf[pl.ds(pl.multiple_of(group * 2 * plane, 2 * plane), 2 * plane), :]

    def encode(group):
        @pl.when(group == z // 2)
        def _():
            weights[0].wait()
            weights[1].wait()
            for copy in weights[2:]:
                copy.start()

        total = jnp.dot(rows_of(gath1, group), enc_w[...], preferred_element_type=f32)
        preact = total + bias_ref[...].reshape(1, -1)
        acts = preact * jax.nn.sigmoid(sharpness * (preact - thr_ref[...].reshape(1, -1)))
        scatter1.project(group, acts, dec_w)

    def feed_hidden(group):
        lhs = rows_of(gath2, group)
        gate_proj, up_proj = (
            lax.dot_general(lhs, mat[...], (((1,), (1,)), ((), ())), preferred_element_type=f32)
            for mat in (gate_w, up_w)
        )
        scatter2.project(group, jax.nn.gelu(gate_proj, approximate=True) * up_proj, down_w)

    block(gath1, me)[...] = res_ref[...]
    gather1.run(encode, scatter1.start_first)
    rebuilt = scatter1.run() + dec_bias_ref[...].reshape(1, -1)
    rebuilt_ref[...] = rebuilt
    block(gath2, me)[...] = rms_scale(rebuilt, pre_gain_ref[...].reshape(1, -1)).astype(bf16)
    for copy in weights[2:]:
        copy.wait()
    gather2.run(feed_hidden, scatter2.start_first)
    ffn_sum = scatter2.run()
    out_ref[...] = (rebuilt_ref[...] + rms_scale(ffn_sum, post_gain_ref[...].reshape(1, -1))).astype(bf16)
    for phase in (gather1, scatter1, gather2, scatter2):
        phase.drain()


def fused_device(
    n,
    residual,
    enc_weight,
    enc_bias,
    threshold,
    dec_weight,
    dec_bias,
    pre_gain,
    gate_weight,
    up_weight,
    down_weight,
    post_gain,
):
    rows, D = residual.shape
    Z = n // 4
    vmem = pl.BlockSpec(memory_space=pltpu.VMEM)
    hbm = pl.BlockSpec(memory_space=pl.ANY)

    def twice(shape, dtype):
        return [pltpu.VMEM(shape, dtype)] * 2

    def sems(count):
        return [pltpu.SemaphoreType.DMA((count,))] * 2

    latents, hidden = enc_weight.shape[1], gate_weight.shape[1]
    return pl.pallas_call(
        functools.partial(kernel, Z, rows),
        out_shape=jax.ShapeDtypeStruct(residual.shape, bf16),
        in_specs=[vmem, hbm, vmem, vmem, hbm, vmem, vmem, hbm, hbm, hbm, vmem],
        out_specs=vmem,
        scratch_shapes=[
            pltpu.VMEM(enc_weight.shape, bf16),
            pltpu.VMEM(dec_weight.shape, bf16),
            pltpu.VMEM(gate_weight.shape[::-1], bf16),
            pltpu.VMEM(up_weight.shape[::-1], bf16),
            pltpu.VMEM(down_weight.shape, bf16),
            *twice((n * rows, D), bf16),
            pltpu.VMEM((Z, 2, rows, D), f32),
            *twice((Z, 2, rows, D), bf16),
            *twice((Z, 2, rows, D), bf16),
            *twice((Z, rows, D), bf16),
            *twice((Z, rows, D), bf16),
            *twice((Z, rows, D), bf16),
            *twice((Z, rows, D), bf16),
            *twice((Z, rows, D), bf16),
            pltpu.VMEM((Z, rows, D), f32),
            pltpu.VMEM((rows, D), f32),
            pltpu.SemaphoreType.DMA((5,)),
            *sems(n),
            *sems(5 * Z),
            *sems(4 * Z * halves_of(D)),
            *sems(4 * Z * halves_of(D)),
        ],
        compiler_params=pltpu.CompilerParams(
            collective_id=0, has_side_effects=True, vmem_limit_bytes=60 * 1024 * 1024
        ),
        cost_estimate=pl.CostEstimate(
            flops=2 * n * rows * D * (2 * latents + 3 * hidden),
            bytes_accessed=2 * D * (2 * latents + 3 * hidden),
            transcendentals=n * rows * (latents + hidden),
        ),
    )(
        residual,
        enc_weight,
        enc_bias,
        threshold,
        dec_weight,
        dec_bias,
        pre_gain,
        gate_weight.T,
        up_weight.T,
        down_weight,
        post_gain,
    )


def solution(mesh):
    n = mesh.shape["latent"]

    def per_device(residual, *rest):
        rows, width = residual.shape
        if n % 8 == 0 and n > 8 and rows % 16 == 0 and width % 128 == 0:
            return fused_device(n, residual, *rest)
        return plain_device(residual, *rest)

    return jax.shard_map(
        per_device,
        mesh=mesh,
        in_specs=(
            P(("parts", "latent"), None),
            P(None, "latent"),
            P("latent"),
            P("latent"),
            P("latent", None),
            P(),
            P(),
            P(None, "latent"),
            P(None, "latent"),
            P("latent", None),
            P(),
        ),
        out_specs=P(("parts", "latent"), None),
        check_vma=False,
    )
```

```python
import functools

import jax
import jax.numpy as jnp
from jax import lax
from jax.experimental import pallas as pl
from jax.experimental.pallas import tpu as pltpu
from jax.sharding import PartitionSpec as P

sharpness = 10.0
epsilon = 1e-06
MESH = pl.DeviceIdType.MESH
f32 = jnp.float32
bf16 = jnp.bfloat16


def rms_scale(values, gain):
    return values * lax.rsqrt(jnp.mean(values * values, axis=-1, keepdims=True) + epsilon) * gain


def plain_device(
    residual,
    enc_weight,
    enc_bias,
    threshold,
    dec_weight,
    dec_bias,
    pre_gain,
    gate_weight,
    up_weight,
    down_weight,
    post_gain,
):
    def encode(block_rows):
        preact = jnp.dot(block_rows, enc_weight, preferred_element_type=f32) + enc_bias
        return (preact * jax.nn.sigmoid(sharpness * (preact - threshold))).astype(bf16)

    def feed_hidden(block_rows):
        gate_proj = jnp.dot(block_rows, gate_weight, preferred_element_type=f32)
        up_proj = jnp.dot(block_rows, up_weight, preferred_element_type=f32)
        return (jax.nn.gelu(gate_proj, approximate=True) * up_proj).astype(bf16)

    def scatter_sum(lhs, rhs):
        return lax.psum_scatter(
            jnp.dot(lhs, rhs, preferred_element_type=f32), "latent", scatter_dimension=0, tiled=True
        )

    latent_acts = encode(lax.all_gather(residual, "latent", axis=0, tiled=True))
    rebuilt = scatter_sum(latent_acts, dec_weight) + dec_bias
    normed = rms_scale(rebuilt, pre_gain).astype(bf16)
    hidden = feed_hidden(lax.all_gather(normed, "latent", axis=0, tiled=True))
    ffn_sum = scatter_sum(hidden, down_weight)
    return (rebuilt + rms_scale(ffn_sum, post_gain)).astype(bf16)


def halves_of(extent):
    return 2 if extent % 256 == 0 else 1


def chunk_of(extent):
    for pieces in (6, 4, 8, 2):
        if extent % (128 * pieces) == 0:
            return extent // pieces
    return extent


def kernel(
    Z,
    rows,
    res_ref,
    enc_hbm,
    bias_ref,
    thr_ref,
    dec_hbm,
    dec_bias_ref,
    pre_gain_ref,
    gate_hbm,
    up_hbm,
    down_hbm,
    post_gain_ref,
    out_ref,
    enc_w,
    dec_w,
    gate_w,
    up_w,
    down_w,
    gath1,
    gath2,
    own_part,
    sib_send1,
    sib_send2,
    sib_recv1,
    sib_recv2,
    x_send1,
    x_send2,
    x_recv1,
    x_recv2,
    z_send1,
    z_send2,
    up_recv1,
    up_recv2,
    dn_recv1,
    dn_recv2,
    kept,
    rebuilt_ref,
    w_sem,
    g_recv1,
    g_recv2,
    g_send1,
    g_send2,
    r_recv1,
    r_recv2,
    r_send1,
    r_send2,
):
    me = lax.axis_index("latent")
    z = me // 4
    x = (me // 2) % 2
    c = me % 2
    D = res_ref.shape[1]
    wide = chunk_of(D)
    halves = halves_of(D)
    half = D // halves
    plane = 4 * rows

    def place(pz, px, pc):
        return pz * 4 + px * 2 + pc

    def order_of(own):
        step = 1 - 2 * (own % 2)
        planes = [own] + [own + side * step * d for d in range(1, Z) for side in (1, -1)]
        return [p for p in planes if 0 <= p < Z]

    arrival = [order_of(own) for own in range(Z)]
    leaving = [[order[1], *order[:1:-1], order[0]] for order in arrival]
    passing = [[order[-1], order[1], *order[-2:1:-1], order[0]] for order in arrival]
    groups = [sorted(range(Z // 2), key=lambda g: (abs(g - own // 2), g)) for own in range(Z)]

    def pick(table, k):
        value = 0
        for own in range(Z):
            for place_in_order in range(len(table[own])):
                value += jnp.where((z == own) & (k == place_in_order), table[own][place_in_order], 0)
        return value

    def block(ref, index):
        return ref.at[pl.ds(pl.multiple_of(index * rows, rows), rows)]

    weights = [
        pltpu.make_async_copy(src, dst, w_sem.at[i])
        for i, (src, dst) in enumerate(
            [(enc_hbm, enc_w), (dec_hbm, dec_w), (gate_hbm, gate_w), (up_hbm, up_w), (down_hbm, down_w)]
        )
    ]
    weights[0].start()
    weights[1].start()

    has_up = z < Z - 1
    has_dn = z > 0
    barrier = pltpu.get_barrier_semaphore()

    def greet(index):
        pl.semaphore_signal(barrier, inc=1, device_id={"latent": index}, device_id_type=MESH)

    greet(place(z, x, 1 - c))
    greet(place(z, 1 - x, c))

    @pl.when(has_up)
    def _():
        greet(place(z + 1, x, c))

    @pl.when(has_dn)
    def _():
        greet(place(z - 1, x, c))

    pl.semaphore_wait(barrier, 2 + (z + Z - 1) // Z + (2 * Z - 2 - z) // Z)

    def send(src, dst, send_sem, recv_sem, index):
        return pltpu.make_async_remote_copy(
            src_ref=src,
            dst_ref=dst,
            send_sem=send_sem,
            recv_sem=recv_sem,
            device_id={"latent": index},
            device_id_type=MESH,
        )

    class Gather:
        def __init__(self, buf, send_sems, recv_sems):
            self.buf, self.send_sems, self.recv_sems = buf, send_sems, recv_sems

        def copy(self, index, slot, target):
            ref = block(self.buf, index)
            return send(ref, ref, self.send_sems.at[slot], self.recv_sems.at[index], target)

        def to_x(self, p):
            return self.copy(place(p, x, c), p, place(z, 1 - x, c))

        def to_up(self, p):
            return self.copy(place(p, x, c), Z + p, place(z + 1, x, c))

        def to_dn(self, p):
            return self.copy(place(p, x, c), 2 * Z + p, place(z - 1, x, c))

        def to_sib(self, p, px):
            return self.copy(place(p, px, c), 3 * Z + 2 * p + px, place(z, x, 1 - c))

        def await_block(self, index):
            self.copy(index, 0, place(z, x, 1 - c)).wait_recv()

        def run(self, compute, before_last):
            self.to_x(z).start()

            @pl.when(has_up)
            def _():
                self.to_up(z).start()

            @pl.when(has_dn)
            def _():
                self.to_dn(z).start()

            self.to_sib(z, x).start()
            toward = 1 - 2 * (z % 2)

            for d in range(1, Z):
                first, second = z + toward * d, z - toward * d
                first_is = (first >= 0) & (first < Z)

                @pl.when(first_is)
                def _():
                    self.pass_on(first)
                    self.to_x(first).start()

                second_is = (second >= 0) & (second < Z)

                @pl.when(second_is)
                def _():
                    self.pass_on(second)

                if d > 1:

                    @pl.when((first - toward >= 0) & (first - toward < Z) & (second + toward >= 0) & (second + toward < Z))
                    def _():
                        self.to_x(second + toward).start()

                @pl.when(second_is & jnp.logical_not(first_is))
                def _():
                    self.to_x(second).start()

            @pl.loop(0, Z // 2)
            def _(g):
                for k in range(Z):

                    @pl.when(g == (0 if k < 2 else 1))
                    def _():
                        p = pick(arrival, k)
                        self.await_block(place(p, 1 - x, c))
                        self.to_sib(p, 1 - x).start()

                group = pick(groups, g)
                for p in (2 * group, 2 * group + 1):
                    for px in range(2):
                        self.await_block(place(p, px, 1 - c))

                @pl.when(g == Z // 2 - 1)
                def _():
                    before_last()

                compute(group)

        def pass_on(self, p):
            self.await_block(place(p, x, c))

            @pl.when((p < z) & has_up)
            def _():
                self.to_up(p).start()

            @pl.when((p > z) & has_dn)
            def _():
                self.to_dn(p).start()

            self.to_sib(p, x).start()

        def drain(self):
            for p in range(Z):
                self.to_x(p).wait_send()
                self.to_sib(p, 0).wait_send()
                self.to_sib(p, 1).wait_send()

                @pl.when(has_up & (p <= z))
                def _():
                    self.to_up(p).wait_send()

                @pl.when(has_dn & (p >= z))
                def _():
                    self.to_dn(p).wait_send()

    class Scatter:
        def __init__(self, sib_send, sib_recv, x_send, x_recv, z_send, up_recv, dn_recv, send_sems, recv_sems):
            self.sib_send, self.sib_recv = sib_send, sib_recv
            self.x_send, self.x_recv = x_send, x_recv
            self.z_send, self.up_recv, self.dn_recv = z_send, up_recv, dn_recv
            self.send_sems, self.recv_sems = send_sems, recv_sems

        def copy(self, src, dst, kind, p, h, target):
            cols = pl.ds(pl.multiple_of(h * half, half), half)
            slot = kind * Z * halves + p * halves + h
            return send(
                src.at[p, :, cols], dst.at[p, :, cols], self.send_sems.at[slot], self.recv_sems.at[slot], target
            )

        def to_sib(self, p):
            return send(
                self.sib_send.at[p], self.sib_recv.at[p], self.send_sems.at[p], self.recv_sems.at[p], place(z, x, 1 - c)
            )

        def to_x(self, p, h):
            return self.copy(self.x_send, self.x_recv, 1, p, h, place(z, 1 - x, c))

        def to_up(self, p, h):
            return self.copy(self.z_send, self.up_recv, 2, p, h, place(z + 1, x, c))

        def to_dn(self, p, h):
            return self.copy(self.z_send, self.dn_recv, 3, p, h, place(z - 1, x, c))

        def project(self, group, acts, weight):
            blocks = [acts[i * rows : (i + 1) * rows] for i in range(8)]
            first = c == 0
            others = [jnp.where(first, blocks[i + 1], blocks[i]) for i in range(0, 8, 2)]
            own = [jnp.where(first, blocks[i], blocks[i + 1]) for i in range(0, 8, 2)]
            lhs = jnp.concatenate(others + own, axis=0).astype(bf16)
            for k in range(D // wide):
                cols = slice(k * wide, (k + 1) * wide)
                term = jnp.dot(lhs, weight[:, cols], preferred_element_type=f32)
                for i in range(4):
                    p = 2 * group + i // 2
                    self.sib_send[p, i % 2, :, cols] = term[i * rows : (i + 1) * rows].astype(bf16)
                    own_part[p, i % 2, :, cols] = term[(4 + i) * rows : (5 + i) * rows]

            self.to_sib(2 * group).start()
            self.to_sib(2 * group + 1).start()

        def start_x(self, j):
            p, h = pick(leaving, j // halves), j % halves
            cols = pl.ds(pl.multiple_of(h * half, half), half)

            @pl.when(h == 0)
            def _():
                self.to_sib(p).wait_recv()

            self.x_send[p, :, cols] = (
                own_part[p, 1 - x, :, cols] + self.sib_recv[p, 1 - x, :, cols].astype(f32)
            ).astype(bf16)
            self.to_x(p, h).start()
            kept[p, :, cols] = own_part[p, x, :, cols] + self.sib_recv[p, x, :, cols].astype(f32)

        def start_first(self):
            for j in range(halves):
                self.start_x(j)

        def run(self):
            for j in range(halves, 2 * halves):
                self.start_x(j)

            @pl.loop(0, Z * halves)
            def _(j):
                @pl.when(j + 2 * halves < Z * halves)
                def _():
                    self.to_x(pick(leaving, j // halves + 1), j % halves).wait_send()
                    self.start_x(j + 2 * halves)

                p, h = pick(passing, j // halves), j % halves
                cols = pl.ds(pl.multiple_of(h * half, half), half)
                self.to_x(p, h).wait_recv()
                kept[p, :, cols] += self.x_recv[p, :, cols].astype(f32)

                @pl.when((p <= z) & has_up)
                def _():
                    self.to_dn(p, h).wait_recv()
                    kept[p, :, cols] += self.dn_recv[p, :, cols].astype(f32)

                @pl.when((p >= z) & has_dn)
                def _():
                    self.to_up(p, h).wait_recv()
                    kept[p, :, cols] += self.up_recv[p, :, cols].astype(f32)

                @pl.when(p != z)
                def _():
                    self.z_send[p, :, cols] = kept[p, :, cols].astype(bf16)

                @pl.when(p < z)
                def _():
                    self.to_dn(p, h).start()

                @pl.when(p > z)
                def _():
                    self.to_up(p, h).start()

            return kept[z]

        def drain(self):
            for p in range(Z):
                self.to_sib(p).wait_send()
                for h in range(halves):

                    @pl.when((p == pick(leaving, 0)) | (p == pick(leaving, Z - 1)))
                    def _():
                        self.to_x(p, h).wait_send()

                    @pl.when(p > z)
                    def _():
                        self.to_up(p, h).wait_send()

                    @pl.when(p < z)
                    def _():
                        self.to_dn(p, h).wait_send()

    gather1 = Gather(gath1, g_send1, g_recv1)
    gather2 = Gather(gath2, g_send2, g_recv2)
    scatter1 = Scatter(
        sib_send1, sib_recv1, x_send1, x_recv1, z_send1, up_recv1, dn_recv1, r_send1, r_recv1
    )
    scatter2 = Scatter(
        sib_send2, sib_recv2, x_send2, x_recv2, z_send2, up_recv2, dn_recv2, r_send2, r_recv2
    )

    def rows_of(buf, group):
        return buf[pl.ds(pl.multiple_of(group * 2 * plane, 2 * plane), 2 * plane), :]

    def encode(group):
        @pl.when(group == z // 2)
        def _():
            weights[0].wait()
            weights[1].wait()
            for copy in weights[2:]:
                copy.start()

        total = jnp.dot(rows_of(gath1, group), enc_w[...], preferred_element_type=f32)
        preact = total + bias_ref[...].reshape(1, -1)
        acts = preact * jax.nn.sigmoid(sharpness * (preact - thr_ref[...].reshape(1, -1)))
        scatter1.project(group, acts, dec_w)

    def feed_hidden(group):
        lhs = rows_of(gath2, group)
        gate_proj, up_proj = (
            lax.dot_general(lhs, mat[...], (((1,), (1,)), ((), ())), preferred_element_type=f32)
            for mat in (gate_w, up_w)
        )
        scatter2.project(group, jax.nn.gelu(gate_proj, approximate=True) * up_proj, down_w)

    block(gath1, me)[...] = res_ref[...]
    gather1.run(encode, scatter1.start_first)
    rebuilt = scatter1.run() + dec_bias_ref[...].reshape(1, -1)
    rebuilt_ref[...] = rebuilt
    block(gath2, me)[...] = rms_scale(rebuilt, pre_gain_ref[...].reshape(1, -1)).astype(bf16)
    for copy in weights[2:]:
        copy.wait()
    gather2.run(feed_hidden, scatter2.start_first)
    ffn_sum = scatter2.run()
    out_ref[...] = (rebuilt_ref[...] + rms_scale(ffn_sum, post_gain_ref[...].reshape(1, -1))).astype(bf16)
    for phase in (gather1, scatter1, gather2, scatter2):
        phase.drain()


def fused_device(
    n,
    residual,
    enc_weight,
    enc_bias,
    threshold,
    dec_weight,
    dec_bias,
    pre_gain,
    gate_weight,
    up_weight,
    down_weight,
    post_gain,
):
    rows, D = residual.shape
    Z = n // 4
    vmem = pl.BlockSpec(memory_space=pltpu.VMEM)
    hbm = pl.BlockSpec(memory_space=pl.ANY)

    def twice(shape, dtype):
        return [pltpu.VMEM(shape, dtype)] * 2

    def sems(count):
        return [pltpu.SemaphoreType.DMA((count,))] * 2

    latents, hidden = enc_weight.shape[1], gate_weight.shape[1]
    return pl.pallas_call(
        functools.partial(kernel, Z, rows),
        out_shape=jax.ShapeDtypeStruct(residual.shape, bf16),
        in_specs=[vmem, hbm, vmem, vmem, hbm, vmem, vmem, hbm, hbm, hbm, vmem],
        out_specs=vmem,
        scratch_shapes=[
            pltpu.VMEM(enc_weight.shape, bf16),
            pltpu.VMEM(dec_weight.shape, bf16),
            pltpu.VMEM(gate_weight.shape[::-1], bf16),
            pltpu.VMEM(up_weight.shape[::-1], bf16),
            pltpu.VMEM(down_weight.shape, bf16),
            *twice((n * rows, D), bf16),
            pltpu.VMEM((Z, 2, rows, D), f32),
            *twice((Z, 2, rows, D), bf16),
            *twice((Z, 2, rows, D), bf16),
            *twice((Z, rows, D), bf16),
            *twice((Z, rows, D), bf16),
            *twice((Z, rows, D), bf16),
            *twice((Z, rows, D), bf16),
            *twice((Z, rows, D), bf16),
            pltpu.VMEM((Z, rows, D), f32),
            pltpu.VMEM((rows, D), f32),
            pltpu.SemaphoreType.DMA((5,)),
            *sems(n),
            *sems(5 * Z),
            *sems(4 * Z * halves_of(D)),
            *sems(4 * Z * halves_of(D)),
        ],
        compiler_params=pltpu.CompilerParams(
            collective_id=0, has_side_effects=True, vmem_limit_bytes=60 * 1024 * 1024
        ),
        cost_estimate=pl.CostEstimate(
            flops=2 * n * rows * D * (2 * latents + 3 * hidden),
            bytes_accessed=2 * D * (2 * latents + 3 * hidden),
            transcendentals=n * rows * (latents + hidden),
        ),
    )(
        residual,
        enc_weight,
        enc_bias,
        threshold,
        dec_weight,
        dec_bias,
        pre_gain,
        gate_weight.T,
        up_weight.T,
        down_weight,
        post_gain,
    )


def solution(mesh):
    n = mesh.shape["latent"]

    def per_device(residual, *rest):
        rows, width = residual.shape
        if n % 8 == 0 and n > 8 and rows % 16 == 0 and width % 128 == 0:
            return fused_device(n, residual, *rest)
        return plain_device(residual, *rest)

    return jax.shard_map(
        per_device,
        mesh=mesh,
        in_specs=(
            P(("parts", "latent"), None),
            P(None, "latent"),
            P("latent"),
            P("latent"),
            P("latent", None),
            P(),
            P(),
            P(None, "latent"),
            P(None, "latent"),
            P("latent", None),
            P(),
        ),
        out_specs=P(("parts", "latent"), None),
        check_vma=False,
    )
```

```python
import functools

import jax
import jax.numpy as jnp
from jax import lax
from jax.experimental import pallas as pl
from jax.experimental.pallas import tpu as pltpu
from jax.sharding import PartitionSpec as P

sharpness = 10.0
epsilon = 1e-06
MESH = pl.DeviceIdType.MESH
f32 = jnp.float32
bf16 = jnp.bfloat16


def rms_scale(values, gain):
    return values * lax.rsqrt(jnp.mean(values * values, axis=-1, keepdims=True) + epsilon) * gain


def plain_device(
    residual,
    enc_weight,
    enc_bias,
    threshold,
    dec_weight,
    dec_bias,
    pre_gain,
    gate_weight,
    up_weight,
    down_weight,
    post_gain,
):
    def encode(block_rows):
        preact = jnp.dot(block_rows, enc_weight, preferred_element_type=f32) + enc_bias
        return (preact * jax.nn.sigmoid(sharpness * (preact - threshold))).astype(bf16)

    def feed_hidden(block_rows):
        gate_proj = jnp.dot(block_rows, gate_weight, preferred_element_type=f32)
        up_proj = jnp.dot(block_rows, up_weight, preferred_element_type=f32)
        return (jax.nn.gelu(gate_proj, approximate=True) * up_proj).astype(bf16)

    def scatter_sum(lhs, rhs):
        return lax.psum_scatter(
            jnp.dot(lhs, rhs, preferred_element_type=f32), "latent", scatter_dimension=0, tiled=True
        )

    latent_acts = encode(lax.all_gather(residual, "latent", axis=0, tiled=True))
    rebuilt = scatter_sum(latent_acts, dec_weight) + dec_bias
    normed = rms_scale(rebuilt, pre_gain).astype(bf16)
    hidden = feed_hidden(lax.all_gather(normed, "latent", axis=0, tiled=True))
    ffn_sum = scatter_sum(hidden, down_weight)
    return (rebuilt + rms_scale(ffn_sum, post_gain)).astype(bf16)


def halves_of(extent):
    return 2 if extent % 256 == 0 else 1


def chunk_of(extent):
    for pieces in (6, 4, 8, 2):
        if extent % (128 * pieces) == 0:
            return extent // pieces
    return extent


def kernel(
    Z,
    rows,
    res_ref,
    enc_hbm,
    bias_ref,
    thr_ref,
    dec_hbm,
    dec_bias_ref,
    pre_gain_ref,
    gate_hbm,
    up_hbm,
    down_hbm,
    post_gain_ref,
    out_ref,
    enc_w,
    dec_w,
    gate_w,
    up_w,
    down_w,
    gath1,
    gath2,
    own_part,
    sib_send1,
    sib_send2,
    sib_recv1,
    sib_recv2,
    x_send1,
    x_send2,
    x_recv1,
    x_recv2,
    z_send1,
    z_send2,
    up_recv1,
    up_recv2,
    dn_recv1,
    dn_recv2,
    kept,
    rebuilt_ref,
    w_sem,
    g_recv1,
    g_recv2,
    g_send1,
    g_send2,
    r_recv1,
    r_recv2,
    r_send1,
    r_send2,
):
    me = lax.axis_index("latent")
    z = me // 4
    x = (me // 2) % 2
    c = me % 2
    D = res_ref.shape[1]
    wide = chunk_of(D)
    halves = halves_of(D)
    half = D // halves
    plane = 4 * rows

    def place(pz, px, pc):
        return pz * 4 + px * 2 + pc

    def order_of(own):
        step = 1 - 2 * (own % 2)
        planes = [own] + [own + side * step * d for d in range(1, Z) for side in (1, -1)]
        return [p for p in planes if 0 <= p < Z]

    arrival = [order_of(own) for own in range(Z)]
    leaving = [[order[1], *order[:1:-1], order[0]] for order in arrival]
    passing = [[order[-1], order[1], *order[-2:1:-1], order[0]] for order in arrival]
    groups = [sorted(range(Z // 2), key=lambda g: (abs(g - own // 2), g)) for own in range(Z)]

    def pick(table, k):
        value = 0
        for own in range(Z):
            for place_in_order in range(len(table[own])):
                value += jnp.where((z == own) & (k == place_in_order), table[own][place_in_order], 0)
        return value

    def block(ref, index):
        return ref.at[pl.ds(pl.multiple_of(index * rows, rows), rows)]

    weights = [
        pltpu.make_async_copy(src, dst, w_sem.at[i])
        for i, (src, dst) in enumerate(
            [(enc_hbm, enc_w), (dec_hbm, dec_w), (gate_hbm, gate_w), (up_hbm, up_w), (down_hbm, down_w)]
        )
    ]
    weights[0].start()
    weights[1].start()

    has_up = z < Z - 1
    has_dn = z > 0
    barrier = pltpu.get_barrier_semaphore()

    def greet(index):
        pl.semaphore_signal(barrier, inc=1, device_id={"latent": index}, device_id_type=MESH)

    greet(place(z, x, 1 - c))
    greet(place(z, 1 - x, c))

    @pl.when(has_up)
    def _():
        greet(place(z + 1, x, c))

    @pl.when(has_dn)
    def _():
        greet(place(z - 1, x, c))

    pl.semaphore_wait(barrier, 2 + (z + Z - 1) // Z + (2 * Z - 2 - z) // Z)

    def send(src, dst, send_sem, recv_sem, index):
        return pltpu.make_async_remote_copy(
            src_ref=src,
            dst_ref=dst,
            send_sem=send_sem,
            recv_sem=recv_sem,
            device_id={"latent": index},
            device_id_type=MESH,
        )

    class Gather:
        def __init__(self, buf, send_sems, recv_sems):
            self.buf, self.send_sems, self.recv_sems = buf, send_sems, recv_sems

        def copy(self, index, slot, target):
            ref = block(self.buf, index)
            return send(ref, ref, self.send_sems.at[slot], self.recv_sems.at[index], target)

        def to_x(self, p):
            return self.copy(place(p, x, c), p, place(z, 1 - x, c))

        def to_up(self, p):
            return self.copy(place(p, x, c), Z + p, place(z + 1, x, c))

        def to_dn(self, p):
            return self.copy(place(p, x, c), 2 * Z + p, place(z - 1, x, c))

        def to_sib(self, p, px):
            return self.copy(place(p, px, c), 3 * Z + 2 * p + px, place(z, x, 1 - c))

        def await_block(self, index):
            self.copy(index, 0, place(z, x, 1 - c)).wait_recv()

        def run(self, compute, before_last):
            self.to_x(z).start()

            @pl.when(has_up)
            def _():
                self.to_up(z).start()

            @pl.when(has_dn)
            def _():
                self.to_dn(z).start()

            self.to_sib(z, x).start()
            toward = 1 - 2 * (z % 2)

            for d in range(1, Z):
                first, second = z + toward * d, z - toward * d
                first_is = (first >= 0) & (first < Z)

                @pl.when(first_is)
                def _():
                    self.pass_on(first)
                    self.to_x(first).start()

                second_is = (second >= 0) & (second < Z)

                @pl.when(second_is)
                def _():
                    self.pass_on(second)

                if d > 1:

                    @pl.when((first - toward >= 0) & (first - toward < Z) & (second + toward >= 0) & (second + toward < Z))
                    def _():
                        self.to_x(second + toward).start()

                @pl.when(second_is & jnp.logical_not(first_is))
                def _():
                    self.to_x(second).start()

            @pl.loop(0, Z // 2)
            def _(g):
                for k in range(Z):

                    @pl.when(g == (0 if k < 2 else 1))
                    def _():
                        p = pick(arrival, k)
                        self.await_block(place(p, 1 - x, c))
                        self.to_sib(p, 1 - x).start()

                group = pick(groups, g)
                for p in (2 * group, 2 * group + 1):
                    for px in range(2):
                        self.await_block(place(p, px, 1 - c))

                @pl.when(g == Z // 2 - 1)
                def _():
                    before_last()

                compute(group)

        def pass_on(self, p):
            self.await_block(place(p, x, c))

            @pl.when((p < z) & has_up)
            def _():
                self.to_up(p).start()

            @pl.when((p > z) & has_dn)
            def _():
                self.to_dn(p).start()

            self.to_sib(p, x).start()

        def drain(self):
            for p in range(Z):
                self.to_x(p).wait_send()
                self.to_sib(p, 0).wait_send()
                self.to_sib(p, 1).wait_send()

                @pl.when(has_up & (p <= z))
                def _():
                    self.to_up(p).wait_send()

                @pl.when(has_dn & (p >= z))
                def _():
                    self.to_dn(p).wait_send()

    class Scatter:
        def __init__(self, sib_send, sib_recv, x_send, x_recv, z_send, up_recv, dn_recv, send_sems, recv_sems):
            self.sib_send, self.sib_recv = sib_send, sib_recv
            self.x_send, self.x_recv = x_send, x_recv
            self.z_send, self.up_recv, self.dn_recv = z_send, up_recv, dn_recv
            self.send_sems, self.recv_sems = send_sems, recv_sems

        def copy(self, src, dst, kind, p, h, target):
            cols = pl.ds(pl.multiple_of(h * half, half), half)
            slot = kind * Z * halves + p * halves + h
            return send(
                src.at[p, :, cols], dst.at[p, :, cols], self.send_sems.at[slot], self.recv_sems.at[slot], target
            )

        def to_sib(self, p):
            return send(
                self.sib_send.at[p], self.sib_recv.at[p], self.send_sems.at[p], self.recv_sems.at[p], place(z, x, 1 - c)
            )

        def to_x(self, p, h):
            return self.copy(self.x_send, self.x_recv, 1, p, h, place(z, 1 - x, c))

        def to_up(self, p, h):
            return self.copy(self.z_send, self.up_recv, 2, p, h, place(z + 1, x, c))

        def to_dn(self, p, h):
            return self.copy(self.z_send, self.dn_recv, 3, p, h, place(z - 1, x, c))

        def project(self, group, acts, weight):
            blocks = [acts[i * rows : (i + 1) * rows] for i in range(8)]
            first = c == 0
            others = [jnp.where(first, blocks[i + 1], blocks[i]) for i in range(0, 8, 2)]
            own = [jnp.where(first, blocks[i], blocks[i + 1]) for i in range(0, 8, 2)]
            lhs = jnp.concatenate(others + own, axis=0).astype(bf16)
            for k in range(D // wide):
                cols = slice(k * wide, (k + 1) * wide)
                term = jnp.dot(lhs, weight[:, cols], preferred_element_type=f32)
                for i in range(4):
                    p = 2 * group + i // 2
                    self.sib_send[p, i % 2, :, cols] = term[i * rows : (i + 1) * rows].astype(bf16)
                    own_part[p, i % 2, :, cols] = term[(4 + i) * rows : (5 + i) * rows]

            self.to_sib(2 * group).start()
            self.to_sib(2 * group + 1).start()

        def start_x(self, j):
            p, h = pick(leaving, j // halves), j % halves
            cols = pl.ds(pl.multiple_of(h * half, half), half)

            @pl.when(h == 0)
            def _():
                self.to_sib(p).wait_recv()

            self.x_send[p, :, cols] = (
                own_part[p, 1 - x, :, cols] + self.sib_recv[p, 1 - x, :, cols].astype(f32)
            ).astype(bf16)
            self.to_x(p, h).start()
            kept[p, :, cols] = own_part[p, x, :, cols] + self.sib_recv[p, x, :, cols].astype(f32)

        def start_first(self):
            for j in range(halves):
                self.start_x(j)

        def run(self):
            @pl.loop(halves, Z * halves)
            def _(j):
                self.start_x(j)

            @pl.loop(0, Z * halves)
            def _(j):
                p, h = pick(passing, j // halves), j % halves
                cols = pl.ds(pl.multiple_of(h * half, half), half)
                self.to_x(p, h).wait_recv()
                kept[p, :, cols] += self.x_recv[p, :, cols].astype(f32)

                @pl.when((p <= z) & has_up)
                def _():
                    self.to_dn(p, h).wait_recv()
                    kept[p, :, cols] += self.dn_recv[p, :, cols].astype(f32)

                @pl.when((p >= z) & has_dn)
                def _():
                    self.to_up(p, h).wait_recv()
                    kept[p, :, cols] += self.up_recv[p, :, cols].astype(f32)

                @pl.when(p != z)
                def _():
                    self.z_send[p, :, cols] = kept[p, :, cols].astype(bf16)

                @pl.when(p < z)
                def _():
                    self.to_dn(p, h).start()

                @pl.when(p > z)
                def _():
                    self.to_up(p, h).start()

            return kept[z]

        def drain(self):
            for p in range(Z):
                self.to_sib(p).wait_send()
                for h in range(halves):
                    self.to_x(p, h).wait_send()

                    @pl.when(p > z)
                    def _():
                        self.to_up(p, h).wait_send()

                    @pl.when(p < z)
                    def _():
                        self.to_dn(p, h).wait_send()

    gather1 = Gather(gath1, g_send1, g_recv1)
    gather2 = Gather(gath2, g_send2, g_recv2)
    scatter1 = Scatter(
        sib_send1, sib_recv1, x_send1, x_recv1, z_send1, up_recv1, dn_recv1, r_send1, r_recv1
    )
    scatter2 = Scatter(
        sib_send2, sib_recv2, x_send2, x_recv2, z_send2, up_recv2, dn_recv2, r_send2, r_recv2
    )

    def rows_of(buf, group):
        return buf[pl.ds(pl.multiple_of(group * 2 * plane, 2 * plane), 2 * plane), :]

    def encode(group):
        @pl.when(group == z // 2)
        def _():
            weights[0].wait()
            weights[1].wait()
            for copy in weights[2:]:
                copy.start()

        total = jnp.dot(rows_of(gath1, group), enc_w[...], preferred_element_type=f32)
        preact = total + bias_ref[...].reshape(1, -1)
        acts = preact * jax.nn.sigmoid(sharpness * (preact - thr_ref[...].reshape(1, -1)))
        scatter1.project(group, acts, dec_w)

    def feed_hidden(group):
        lhs = rows_of(gath2, group)
        gate_proj, up_proj = (
            lax.dot_general(lhs, mat[...], (((1,), (1,)), ((), ())), preferred_element_type=f32)
            for mat in (gate_w, up_w)
        )
        scatter2.project(group, jax.nn.gelu(gate_proj, approximate=True) * up_proj, down_w)

    block(gath1, me)[...] = res_ref[...]
    gather1.run(encode, scatter1.start_first)
    rebuilt = scatter1.run() + dec_bias_ref[...].reshape(1, -1)
    rebuilt_ref[...] = rebuilt
    block(gath2, me)[...] = rms_scale(rebuilt, pre_gain_ref[...].reshape(1, -1)).astype(bf16)
    for copy in weights[2:]:
        copy.wait()
    gather2.run(feed_hidden, scatter2.start_first)
    ffn_sum = scatter2.run()
    out_ref[...] = (rebuilt_ref[...] + rms_scale(ffn_sum, post_gain_ref[...].reshape(1, -1))).astype(bf16)
    for phase in (gather1, scatter1, gather2, scatter2):
        phase.drain()


def fused_device(
    n,
    residual,
    enc_weight,
    enc_bias,
    threshold,
    dec_weight,
    dec_bias,
    pre_gain,
    gate_weight,
    up_weight,
    down_weight,
    post_gain,
):
    rows, D = residual.shape
    Z = n // 4
    vmem = pl.BlockSpec(memory_space=pltpu.VMEM)
    hbm = pl.BlockSpec(memory_space=pl.ANY)

    def twice(shape, dtype):
        return [pltpu.VMEM(shape, dtype)] * 2

    def sems(count):
        return [pltpu.SemaphoreType.DMA((count,))] * 2

    latents, hidden = enc_weight.shape[1], gate_weight.shape[1]
    return pl.pallas_call(
        functools.partial(kernel, Z, rows),
        out_shape=jax.ShapeDtypeStruct(residual.shape, bf16),
        in_specs=[vmem, hbm, vmem, vmem, hbm, vmem, vmem, hbm, hbm, hbm, vmem],
        out_specs=vmem,
        scratch_shapes=[
            pltpu.VMEM(enc_weight.shape, bf16),
            pltpu.VMEM(dec_weight.shape, bf16),
            pltpu.VMEM(gate_weight.shape[::-1], bf16),
            pltpu.VMEM(up_weight.shape[::-1], bf16),
            pltpu.VMEM(down_weight.shape, bf16),
            *twice((n * rows, D), bf16),
            pltpu.VMEM((Z, 2, rows, D), f32),
            *twice((Z, 2, rows, D), bf16),
            *twice((Z, 2, rows, D), bf16),
            *twice((Z, rows, D), bf16),
            *twice((Z, rows, D), bf16),
            *twice((Z, rows, D), bf16),
            *twice((Z, rows, D), bf16),
            *twice((Z, rows, D), bf16),
            pltpu.VMEM((Z, rows, D), f32),
            pltpu.VMEM((rows, D), f32),
            pltpu.SemaphoreType.DMA((5,)),
            *sems(n),
            *sems(5 * Z),
            *sems(4 * Z * halves_of(D)),
            *sems(4 * Z * halves_of(D)),
        ],
        compiler_params=pltpu.CompilerParams(
            collective_id=0, has_side_effects=True, vmem_limit_bytes=60 * 1024 * 1024
        ),
        cost_estimate=pl.CostEstimate(
            flops=2 * n * rows * D * (2 * latents + 3 * hidden),
            bytes_accessed=2 * D * (2 * latents + 3 * hidden),
            transcendentals=n * rows * (latents + hidden),
        ),
    )(
        residual,
        enc_weight,
        enc_bias,
        threshold,
        dec_weight,
        dec_bias,
        pre_gain,
        gate_weight.T,
        up_weight.T,
        down_weight,
        post_gain,
    )


def solution(mesh):
    n = mesh.shape["latent"]

    def per_device(residual, *rest):
        rows, width = residual.shape
        if n % 8 == 0 and n > 8 and rows % 16 == 0 and width % 128 == 0:
            return fused_device(n, residual, *rest)
        return plain_device(residual, *rest)

    return jax.shard_map(
        per_device,
        mesh=mesh,
        in_specs=(
            P(("parts", "latent"), None),
            P(None, "latent"),
            P("latent"),
            P("latent"),
            P("latent", None),
            P(),
            P(),
            P(None, "latent"),
            P(None, "latent"),
            P("latent", None),
            P(),
        ),
        out_specs=P(("parts", "latent"), None),
        check_vma=False,
    )
```
